256 devices in a mesh: expert: 8 (over z), dp: 32 (over y, x, core).
Axes of the slice: x: 4, y: 4, z: 8, core: 2. Of those that a mesh axis runs over, the one named last changes fastest.
Arguments:
- grads: bfloat16 [32, 3, 768, 2048], P('expert', None, 'dp'), may hold values from -5000 to 5000
- momentum: bfloat16 [32, 3, 768, 2048], P('expert', None, 'dp'), may hold values from -50 to 50
Outputs:
- new_momentum: bfloat16 [32, 3, 768, 2048], P('expert', None, 'dp')
- update: bfloat16 [32, 3, 768, 2048], P('expert', None, 'dp')
The draws below stay inside these ranges and needn't reach their ends.
All inputs are finite; a program needn't handle non-finite values.
Results may differ from the reference program's by a relative error of at most 0.015.
Values may be sent and summed in bfloat16 or wider, within the bound.
A program may use at most 64 MiB of HBM per device.

```python
import math
import jax
import jax.numpy as jnp
from jax import lax

D = 2048
F = 768
ITERS = 2
EXPERTS = 32


def draw_grads(key, part):
    key = jax.random.fold_in(key, 11)
    keys = jax.random.split(key, 5)
    ramp = (jnp.arange(F, dtype=jnp.float32) / F).reshape(1, 1, F, 1)
    rough = jax.random.uniform(keys[0], (1, 1, F, 1), jnp.float32)
    rows = 10.0 ** (0.25 * ramp + 0.75 * rough)
    cols = 10.0 ** jax.random.uniform(keys[1], (EXPERTS, 3, 1, D), jnp.float32)
    steady = (1.0 + 2.0 * jnp.arange(EXPERTS, dtype=jnp.float32) / max(EXPERTS - 1, 1)).reshape(EXPERTS, 1, 1, 1)
    jitter = 10.0 ** (0.5 * jax.random.uniform(keys[4], (EXPERTS, 1, 1, 1), jnp.float32))
    rising = steady * jitter
    base = jnp.clip(jax.random.normal(keys[2], (EXPERTS, 3, F, D), jnp.float32), -5.0, 5.0)
    return (base * rows * cols * rising).astype(jnp.bfloat16)


def draw_momentum(key, part):
    key = jax.random.fold_in(key, 23)
    keys = jax.random.split(key, 3)
    rows = 10.0 ** jax.random.uniform(keys[0], (EXPERTS, 3, F, 1), jnp.float32, -0.5, 0.5)
    cols = 10.0 ** jax.random.uniform(keys[1], (EXPERTS, 3, 1, D), jnp.float32, -0.5, 0.5)
    base = jnp.clip(jax.random.normal(keys[2], (EXPERTS, 3, F, D), jnp.float32), -5.0, 5.0)
    return (base * rows * cols).astype(jnp.bfloat16)


def setup_inputs(seed: int = 0) -> dict:
    key_of = jax.random.split(jax.random.key(seed), 3)
    return {
        "grads": draw_grads(jax.random.fold_in(key_of[2], 71), 0),
        "momentum": draw_momentum(jax.random.fold_in(key_of[2], 71), 0),
    }


lin_coef = 3.4445
cub_coef = -4.775
quint_coef = 2.0315
epsilon = 1e-07
momentum_rate = 0.95

def orthogonal(matrix):
    wide = matrix.astype(jnp.float32)
    norm_value = jnp.sqrt(jnp.sum(wide * wide)) + epsilon
    iterate = (wide / norm_value).astype(jnp.bfloat16)
    for step in range(ITERS):
        gram = jnp.dot(iterate, iterate.T, preferred_element_type=jnp.float32).astype(jnp.bfloat16)
        square = jnp.dot(gram, gram, preferred_element_type=jnp.float32)
        mix = (cub_coef * gram.astype(jnp.float32) + quint_coef * square).astype(jnp.bfloat16)
        iterate = (lin_coef * iterate.astype(jnp.float32) + jnp.dot(mix, iterate, preferred_element_type=jnp.float32)).astype(jnp.bfloat16)
    return iterate

def reference(grads, momentum):
    wide_grads = grads.astype(jnp.float32)
    total = jnp.sum(wide_grads * wide_grads)
    count = grads.shape[0] * grads.shape[1] * grads.shape[2] * grads.shape[3]
    clip = 1.0 / jnp.maximum(jnp.sqrt(total / count), 1.0)
    moment = momentum_rate * momentum.astype(jnp.float32) + clip * wide_grads
    lead = (clip * wide_grads + momentum_rate * moment).astype(jnp.bfloat16)
    flat = lead.reshape(-1, F, D)
    ortho = lax.map(orthogonal, flat)
    scale_value = 0.2 * math.sqrt(max(F, D))
    update = (scale_value * ortho.astype(jnp.float32)).astype(jnp.bfloat16).reshape(grads.shape)
    return (moment.astype(jnp.bfloat16), update)
```

```python
import functools
import math

import jax
import jax.numpy as jnp
from jax import lax
from jax.experimental import pallas as pl
from jax.experimental.pallas import tpu as pltpu
from jax.sharding import PartitionSpec as P

lin_coef = 3.4445
cub_coef = -4.775
quint_coef = 2.0315
epsilon = 1e-07
momentum_rate = 0.95

MESH = pl.DeviceIdType.MESH
F32 = jnp.float32
BF16 = jnp.bfloat16

SIDE = 4
CHIPS = SIDE * SIDE
PLANES = 8
DP = 2 * CHIPS
MATS = 12
ROWS = 24
WIDTH = 2048
FULL = ROWS * DP
CHUNKS = 4
COLS = WIDTH // CHUNKS
HALF = COLS // 2
PIECE = 2 * ROWS
SUM_PEERS = 16


def owner_of(k):
    y = k // (SIDE - 1)
    x = lax.rem(y + 1 + lax.rem(k, SIDE - 1), SIDE)
    return (y * SIDE + x) * 2


def stack_halves(wide):
    return jnp.concatenate([wide[:, :HALF], wide[:, HALF:]], axis=0)


def kernel(
    g_hbm, m_hbm, nm_hbm, up_hbm,
    g_v, m_v, nm_v, up_v, lead, recv, full, acc, gram, mix, prod, mix2, norm_sq, outgoing, returned, part_a, part_b,
    g_sem, m_sem, out_sem, sum_send, sum_recv, lead_send, lead_recv, ret_send, ret_recv,
):
    z = lax.axis_index("expert")
    me = lax.axis_index("dp")
    chip = me // 2
    core = lax.rem(me, 2)
    my_y = chip // SIDE
    my_x = lax.rem(chip, SIDE)
    my_j = lax.rem(my_x - my_y - 1 + 2 * SIDE, SIDE)
    is_owner = jnp.logical_and(core == 0, my_j < SIDE - 1)
    my_k = my_y * (SIDE - 1) + my_j

    line = z * 2 + core

    def peer_a(i):
        p = lax.rem(line + i, SUM_PEERS)
        return (p // 2, chip * 2 + lax.rem(p, 2))

    def peer_b(i):
        p = lax.rem(chip + i, SUM_PEERS)
        return (z, p * 2 + core)

    for k in range(4):
        part = pl.ds(3 * k, 3)
        pltpu.make_async_copy(g_hbm.at[part], g_v.at[part], g_sem.at[k]).start()
    load_m = pltpu.make_async_copy(m_hbm, m_v, m_sem)
    load_m.start()

    barrier = pltpu.get_barrier_semaphore()

    def greet(i, carry):
        pl.semaphore_signal(barrier, inc=1, device_id=peer_a(i), device_id_type=MESH)
        pl.semaphore_signal(barrier, inc=1, device_id=peer_b(i), device_id_type=MESH)
        return carry

    lax.fori_loop(1, SUM_PEERS, greet, 0)

    total = jnp.zeros((8, 128), F32)
    for k in range(4):
        part = pl.ds(3 * k, 3)
        pltpu.make_async_copy(g_hbm.at[part], g_v.at[part], g_sem.at[k]).wait()

        def squares(i, carry):
            wide = g_v[i // 4, :, pl.ds(pl.multiple_of(lax.rem(i, 4) * COLS, COLS), COLS)].astype(F32)
            wide = wide * wide
            wide = wide[0:8] + wide[8:16] + wide[16:24]
            wide = wide[:, 0:256] + wide[:, 256:512]
            return carry + (wide[:, 0:128] + wide[:, 128:256])

        total = lax.fori_loop(12 * k, 12 * k + 12, squares, total, unroll=4)

    pl.semaphore_wait(barrier, 2 * (SUM_PEERS - 1))

    def exchange(total, part, slot, peer, stage):
        part[slot] = total

        def send(i, carry):
            pltpu.make_async_remote_copy(
                src_ref=part.at[slot], dst_ref=part.at[slot], send_sem=sum_send.at[stage], recv_sem=sum_recv.at[stage],
                device_id=peer(i), device_id_type=MESH,
            ).start()
            return carry

        lax.fori_loop(1, SUM_PEERS, send, 0)
        others = part.at[pl.ds(0, SUM_PEERS - 1)]
        pltpu.make_async_copy(others, others, sum_recv.at[stage]).wait()
        return jnp.sum(part[...], axis=0)

    total = exchange(total, part_a, line, peer_a, 0)
    total = exchange(total, part_b, chip, peer_b, 1)
    count = MATS * PLANES * FULL * WIDTH
    mean = jnp.sum(total, axis=(0, 1), keepdims=True) / count
    clip = 1.0 / jnp.maximum(jnp.sqrt(mean), 1.0)

    load_m.wait()

    def send_chunk(c, carry):
        columns = pl.ds(pl.multiple_of(c * COLS, COLS), COLS)

        def send_one(i, carry):
            k = lax.rem(i + me, MATS)
            dest = owner_of(k)
            scaled = clip * g_v[k, :, columns].astype(F32)
            moment = momentum_rate * m_v[k, :, columns].astype(F32) + scaled
            piece = stack_halves(scaled + momentum_rate * moment).astype(BF16)
            lead[c, k] = piece

            @pl.when(dest == me)
            def _():
                recv[c, me] = piece

            @pl.when(dest != me)
            def _():
                pltpu.make_async_remote_copy(
                    src_ref=lead.at[c, k], dst_ref=recv.at[c, me], send_sem=lead_send, recv_sem=lead_recv.at[c],
                    device_id=(z, dest), device_id_type=MESH,
                ).start()

            return carry

        return lax.fori_loop(0, MATS, send_one, carry)

    lax.fori_loop(0, CHUNKS, send_chunk, 0)

    def momentum_step(i, carry):
        k = i // CHUNKS
        columns = pl.ds(pl.multiple_of(lax.rem(i, CHUNKS) * COLS, COLS), COLS)
        scaled = clip * g_v[k, :, columns].astype(F32)
        nm_v[k, :, columns] = (momentum_rate * m_v[k, :, columns].astype(F32) + scaled).astype(BF16)
        return carry

    lax.fori_loop(0, MATS * CHUNKS, momentum_step, 0)
    store_nm = pltpu.make_async_copy(nm_v, nm_hbm, out_sem.at[0])
    store_nm.start()

    @pl.when(is_owner)
    def _():
        norm_sq[...] = jnp.zeros_like(norm_sq)

        def collect(c, carry):
            others = recv.at[c, pl.ds(0, DP - 1)]
            pltpu.make_async_copy(others, others, lead_recv.at[c]).wait()
            left = pl.ds(pl.multiple_of(c * COLS, COLS), HALF)
            right = pl.ds(pl.multiple_of(c * COLS + HALF, HALF), HALF)

            def unpack(j, total):
                one = recv[c, 2 * j].astype(F32)
                two = recv[c, 2 * j + 1].astype(F32)
                rows = pl.ds(pl.multiple_of(j * PIECE, PIECE), PIECE)
                full[rows, left] = jnp.concatenate([one[:ROWS], two[:ROWS]], axis=0).astype(BF16)
                full[rows, right] = jnp.concatenate([one[ROWS:], two[ROWS:]], axis=0).astype(BF16)
                both = one * one + two * two
                both = both[:, :128] + both[:, 128:]
                return total + (both[0:8] + both[8:16] + both[16:24] + both[24:32] + both[32:40] + both[40:48])

            total = lax.fori_loop(0, DP // 2, unpack, jnp.zeros((8, 128), F32))
            norm_sq[...] += total
            columns = pl.ds(pl.multiple_of(c * COLS, COLS), COLS)
            for n in range(3):
                rows = pl.ds(256 * n, 256)
                new = lax.dot_general(
                    full[:, columns], full[rows, columns], (((1,), (1,)), ((), ())), preferred_element_type=F32
                )

                @pl.when(c == 0)
                def _():
                    acc[:, rows] = new

                @pl.when(c != 0)
                def _():
                    acc[:, rows] += new

            return carry

        lax.fori_loop(0, CHUNKS, collect, 0)

        norm = jnp.sqrt(jnp.sum(norm_sq[...], axis=(0, 1), keepdims=True)) + epsilon
        inverse = 1.0 / norm
        gram[...] = (acc[...] * inverse * inverse).astype(BF16)

        def product(left, right, n):
            return jnp.dot(left[...], right[:, pl.ds(256 * n, 256)], preferred_element_type=F32)

        def block(ref, n):
            return ref[:, pl.ds(256 * n, 256)].astype(F32)

        for n in range(3):
            cols = pl.ds(256 * n, 256)
            mix[:, cols] = (cub_coef * block(gram, n) + quint_coef * product(gram, gram, n)).astype(BF16)
        for n in range(3):
            cols = pl.ds(256 * n, 256)
            new = product(mix, gram, n)
            prod[:, cols] = new.astype(BF16)
            acc[:, cols] = lin_coef * lin_coef * block(gram, n) + 2.0 * lin_coef * new
        for n in range(3):
            cols = pl.ds(256 * n, 256)
            gram[:, cols] = (acc[:, cols] + product(mix, prod, n)).astype(BF16)
        for n in range(3):
            cols = pl.ds(256 * n, 256)
            mix2[:, cols] = (cub_coef * block(gram, n) + quint_coef * product(gram, gram, n)).astype(BF16)
        for n in range(3):
            cols = pl.ds(256 * n, 256)
            prod[:, cols] = (lin_coef * (block(mix, n) + block(mix2, n)) + product(mix2, mix, n)).astype(BF16)

        scale = inverse * (0.2 * math.sqrt(max(FULL, WIDTH)))

        def give_back(c, carry):
            for half in range(2):
                columns = pl.ds(pl.multiple_of(c * COLS + half * HALF, HALF), HALF)
                right = full[:, columns]
                new = jnp.dot(prod[...], right, preferred_element_type=F32)
                new = (new + lin_coef * lin_coef * right.astype(F32)) * scale
                for d in range(0, DP, 2):
                    rows = slice(half * ROWS, half * ROWS + ROWS)
                    outgoing[c, d, rows] = new[d * ROWS : (d + 1) * ROWS].astype(BF16)
                    outgoing[c, d + 1, rows] = new[(d + 1) * ROWS : (d + 2) * ROWS].astype(BF16)

            returned[c, my_k] = outgoing[c, me]

            def send(i, carry):
                dest = lax.rem(me + i, DP)
                pltpu.make_async_remote_copy(
                    src_ref=outgoing.at[c, dest], dst_ref=returned.at[c, my_k], send_sem=ret_send,
                    recv_sem=ret_recv.at[c], device_id=(z, dest), device_id_type=MESH,
                ).start()
                return carry

            return lax.fori_loop(1, DP, send, carry)

        lax.fori_loop(0, CHUNKS, give_back, 0)

    def finish(c, carry):
        @pl.when(is_owner)
        def _():
            others = returned.at[c, pl.ds(0, MATS - 1)]
            pltpu.make_async_copy(others, others, ret_recv.at[c]).wait()

        @pl.when(jnp.logical_not(is_owner))
        def _():
            every = returned.at[c]
            pltpu.make_async_copy(every, every, ret_recv.at[c]).wait()

        left = pl.ds(pl.multiple_of(c * COLS, COLS), HALF)
        right = pl.ds(pl.multiple_of(c * COLS + HALF, HALF), HALF)

        def unpack(k, carry):
            piece = returned[c, k].astype(F32)
            up_v[k, :, left] = piece[:ROWS].astype(BF16)
            up_v[k, :, right] = piece[ROWS:].astype(BF16)
            return carry

        return lax.fori_loop(0, MATS, unpack, carry)

    lax.fori_loop(0, CHUNKS, finish, 0)
    store_up = pltpu.make_async_copy(up_v, up_hbm, out_sem.at[1])
    store_up.start()

    for stage, part in ((0, part_a), (1, part_b)):
        others = part.at[pl.ds(0, SUM_PEERS - 1)]
        pltpu.make_async_copy(others, others, sum_send.at[stage]).wait()

    @pl.when(is_owner)
    def _():
        others = lead.at[:, pl.ds(0, MATS - 1)]
        pltpu.make_async_copy(others, others, lead_send).wait()
        others = outgoing.at[:, pl.ds(0, DP - 1)]
        pltpu.make_async_copy(others, others, ret_send).wait()

    @pl.when(jnp.logical_not(is_owner))
    def _():
        pltpu.make_async_copy(lead, lead, lead_send).wait()

    store_nm.wait()
    store_up.wait()


def shards(grads, momentum):
    shape = grads.shape
    flat = (MATS, ROWS, WIDTH)
    out = jax.ShapeDtypeStruct(flat, BF16)
    square = (FULL, FULL)
    new_momentum, update = pl.pallas_call(
        kernel,
        out_shape=(out, out),
        in_specs=[pl.BlockSpec(memory_space=pl.ANY)] * 2,
        out_specs=(pl.BlockSpec(memory_space=pl.ANY),) * 2,
        scratch_shapes=[
            pltpu.VMEM(flat, BF16),
            pltpu.VMEM(flat, BF16),
            pltpu.VMEM(flat, BF16),
            pltpu.VMEM(flat, BF16),
            pltpu.VMEM((CHUNKS, MATS, PIECE, HALF), BF16),
            pltpu.VMEM((CHUNKS, DP, PIECE, HALF), BF16),
            pltpu.VMEM((FULL, WIDTH), BF16),
            pltpu.VMEM(square, F32),
            pltpu.VMEM(square, BF16),
            pltpu.VMEM(square, BF16),
            pltpu.VMEM(square, BF16),
            pltpu.VMEM(square, BF16),
            pltpu.VMEM((8, 128), F32),
            pltpu.VMEM((CHUNKS, DP, PIECE, HALF), BF16),
            pltpu.VMEM((CHUNKS, MATS, PIECE, HALF), BF16),
            pltpu.VMEM((SUM_PEERS, 8, 128), F32),
            pltpu.VMEM((SUM_PEERS, 8, 128), F32),
            pltpu.SemaphoreType.DMA((4,)),
            pltpu.SemaphoreType.DMA,
            pltpu.SemaphoreType.DMA((2,)),
            pltpu.SemaphoreType.DMA((2,)),
            pltpu.SemaphoreType.DMA((2,)),
            pltpu.SemaphoreType.DMA,
            pltpu.SemaphoreType.DMA((CHUNKS,)),
            pltpu.SemaphoreType.DMA,
            pltpu.SemaphoreType.DMA((CHUNKS,)),
        ],
        compiler_params=pltpu.CompilerParams(
            collective_id=0, has_side_effects=True, vmem_limit_bytes=48 * 1024 * 1024
        ),
        name="muon_step",
    )(grads.reshape(flat), momentum.reshape(flat))
    return new_momentum.reshape(shape), update.reshape(shape)


def solution(mesh):
    placed = (P("expert", None, "dp", None), P("expert", None, "dp", None))
    return jax.shard_map(
        shards,
        mesh=mesh,
        in_specs=placed,
        out_specs=(P("expert", None, "dp", None), P("expert", None, "dp", None)),
        check_vma=False,
    )
```

```python
import functools
import math

import jax
import jax.numpy as jnp
from jax import lax
from jax.experimental import pallas as pl
from jax.experimental.pallas import tpu as pltpu
from jax.sharding import PartitionSpec as P

lin_coef = 3.4445
cub_coef = -4.775
quint_coef = 2.0315
epsilon = 1e-07
momentum_rate = 0.95

MESH = pl.DeviceIdType.MESH
F32 = jnp.float32
BF16 = jnp.bfloat16

SIDE = 4
CHIPS = SIDE * SIDE
PLANES = 8
DP = 2 * CHIPS
MATS = 12
ROWS = 24
WIDTH = 2048
FULL = ROWS * DP
COLS = 512
NARROW = 256
PIECE = 2 * ROWS
SUM_PEERS = 16
GATHER = ((0, NARROW), (NARROW, NARROW), (512, COLS), (1024, COLS), (1536, COLS))
SPREAD = ((0, NARROW), (512, COLS), (1024, COLS), (1536, COLS), (NARROW, NARROW))


def owner_of(k):
    y = k // (SIDE - 1)
    x = lax.rem(y + 1 + lax.rem(k, SIDE - 1), SIDE)
    return (y * SIDE + x) * 2


def stack_halves(wide):
    half = wide.shape[1] // 2
    return jnp.concatenate([wide[:, :half], wide[:, half:]], axis=0)


def pieces(count, columns):
    return pltpu.VMEM((count, PIECE, columns // 2), BF16)


def kernel(
    g_hbm, m_hbm, nm_hbm, up_hbm,
    g_v, m_v, nm_v, up_v, raw, recv_g, recv_m, leads, recvs, full, acc, gram, mix, prod, mix2, outgoing, returned, part_a, part_b,
    g_sem, m_sem, out_sem, sum_send, sum_recv, raw_send, raw_recv, lead_send, lead_recv, ret_send, ret_recv,
):
    z = lax.axis_index("expert")
    me = lax.axis_index("dp")
    chip = me // 2
    core = lax.rem(me, 2)
    my_y = chip // SIDE
    my_x = lax.rem(chip, SIDE)
    my_j = lax.rem(my_x - my_y - 1 + 2 * SIDE, SIDE)
    is_owner = jnp.logical_and(core == 0, my_j < SIDE - 1)
    my_k = my_y * (SIDE - 1) + my_j

    line = z * 2 + core

    def peer_a(i):
        p = lax.rem(line + i, SUM_PEERS)
        return (p // 2, chip * 2 + lax.rem(p, 2))

    def peer_b(i):
        p = lax.rem(chip + i, SUM_PEERS)
        return (z, p * 2 + core)

    for k in range(4):
        part = pl.ds(3 * k, 3)
        pltpu.make_async_copy(g_hbm.at[part], g_v.at[part], g_sem.at[k]).start()
    load_m = pltpu.make_async_copy(m_hbm, m_v, m_sem)
    load_m.start()

    barrier = pltpu.get_barrier_semaphore()
    for i in range(1, SUM_PEERS):
        pl.semaphore_signal(barrier, inc=1, device_id=peer_a(i), device_id_type=MESH)
        pl.semaphore_signal(barrier, inc=1, device_id=peer_b(i), device_id_type=MESH)

    @pl.when(is_owner)
    def _():
        for i in range(1, CHIPS):
            other = (z, lax.rem(chip + i, CHIPS) * 2 + 1)
            pl.semaphore_signal(barrier, inc=1, device_id=other, device_id_type=MESH)

    total = jnp.zeros((8, 128), F32)
    for k in range(4):
        part = pl.ds(3 * k, 3)
        pltpu.make_async_copy(g_hbm.at[part], g_v.at[part], g_sem.at[k]).wait()

        def squares(i, carry):
            wide = g_v[i // 4, :, pl.ds(pl.multiple_of(lax.rem(i, 4) * COLS, COLS), COLS)].astype(F32)
            wide = wide * wide
            wide = wide[0:8] + wide[8:16] + wide[16:24]
            wide = wide[:, 0:256] + wide[:, 256:512]
            return carry + (wide[:, 0:128] + wide[:, 128:256])

        total = lax.fori_loop(12 * k, 12 * k + 12, squares, total, unroll=4)

    others_owning = jnp.where(my_j < SIDE - 1, MATS - 1, MATS)
    pl.semaphore_wait(barrier, 2 * (SUM_PEERS - 1) + jnp.where(core == 1, others_owning, 0))

    def send_sum(total, part, slot, peer, stage):
        part[slot] = total
        for i in range(1, SUM_PEERS):
            pltpu.make_async_remote_copy(
                src_ref=part.at[slot], dst_ref=part.at[slot], send_sem=sum_send.at[stage], recv_sem=sum_recv.at[stage],
                device_id=peer(i), device_id_type=MESH,
            ).start()

    def take_sum(part, stage):
        others = part.at[pl.ds(0, SUM_PEERS - 1)]
        pltpu.make_async_copy(others, others, sum_recv.at[stage]).wait()
        return jnp.sum(part[...], axis=0)

    def push(piece, buffer, slot, landing, k, send_sem, recv_sem):
        dest = owner_of(k)
        buffer[slot] = piece

        @pl.when(dest == me)
        def _():
            landing[me] = piece

        @pl.when(dest != me)
        def _():
            pltpu.make_async_remote_copy(
                src_ref=buffer.at[slot], dst_ref=landing.at[me], send_sem=send_sem, recv_sem=recv_sem,
                device_id=(z, dest), device_id_type=MESH,
            ).start()

    send_sum(total, part_a, line, peer_a, 0)
    load_m.wait()

    def send_raw(i, carry):
        k = lax.rem(i + me, MATS)
        push(stack_halves(g_v[k, :, :NARROW].astype(F32)).astype(BF16), raw, k, recv_g, k, raw_send, raw_recv.at[0])
        push(stack_halves(m_v[k, :, :NARROW].astype(F32)).astype(BF16), raw, MATS + k, recv_m, k, raw_send, raw_recv.at[1])
        return carry

    lax.fori_loop(0, MATS // 2, send_raw, 0)
    total = take_sum(part_a, 0)
    send_sum(total, part_b, chip, peer_b, 1)
    lax.fori_loop(MATS // 2, MATS, send_raw, 0)
    total = take_sum(part_b, 1)
    count = MATS * PLANES * FULL * WIDTH
    mean = jnp.sum(total, axis=(0, 1), keepdims=True) / count
    clip = 1.0 / jnp.maximum(jnp.sqrt(mean), 1.0)

    def combine(g, m):
        scaled = clip * g.astype(F32)
        moment = momentum_rate * m.astype(F32) + scaled
        return moment, scaled + momentum_rate * moment

    for c in range(1, len(GATHER)):
        columns = pl.ds(*GATHER[c])

        def send_lead(i, carry, columns=columns, c=c):
            k = lax.rem(i + me, MATS)
            piece = stack_halves(combine(g_v[k, :, columns], m_v[k, :, columns])[1]).astype(BF16)
            push(piece, leads[c - 1], k, recvs[c - 1], k, lead_send.at[c - 1], lead_recv.at[c - 1])
            return carry

        lax.fori_loop(0, MATS, send_lead, 0)

    def momentum_step(i, carry):
        k = i // 4
        columns = pl.ds(pl.multiple_of(lax.rem(i, 4) * COLS, COLS), COLS)
        nm_v[k, :, columns] = combine(g_v[k, :, columns], m_v[k, :, columns])[0].astype(BF16)
        return carry

    lax.fori_loop(0, 4 * MATS, momentum_step, 0, unroll=4)
    store_nm = pltpu.make_async_copy(nm_v, nm_hbm, out_sem.at[0])
    store_nm.start()

    @pl.when(is_owner)
    def _():
        def unpack(one, two, j, start, total):
            half = one.shape[1]
            rows = pl.ds(pl.multiple_of(j * PIECE, PIECE), PIECE)
            full[rows, pl.ds(start, half)] = jnp.concatenate([one[:ROWS], two[:ROWS]], axis=0).astype(BF16)
            full[rows, pl.ds(start + half, half)] = jnp.concatenate([one[ROWS:], two[ROWS:]], axis=0).astype(BF16)
            both = one * one + two * two
            if half == 256:
                both = both[:, :128] + both[:, 128:]
            return total + (both[0:8] + both[8:16] + both[16:24] + both[24:32] + both[32:40] + both[40:48])

        def lower(n):
            return pl.ds(256 * n, FULL - 256 * n), pl.ds(256 * n, 256)

        def grams(columns):
            for n in range(3):
                low, cols = lower(n)
                new = lax.dot_general(
                    full[low, columns], full[cols, columns], (((1,), (1,)), ((), ())), preferred_element_type=F32
                )
                yield low, cols, new

        for stage, landing in ((0, recv_g), (1, recv_m)):
            others = landing.at[pl.ds(0, DP - 1)]
            pltpu.make_async_copy(others, others, raw_recv.at[stage]).wait()

        def unpack_raw(j, total):
            one = combine(recv_g[2 * j], recv_m[2 * j])[1].astype(BF16).astype(F32)
            two = combine(recv_g[2 * j + 1], recv_m[2 * j + 1])[1].astype(BF16).astype(F32)
            return unpack(one, two, j, 0, total)

        squared = lax.fori_loop(0, DP // 2, unpack_raw, jnp.zeros((8, 128), F32), unroll=4)
        for low, cols, new in grams(pl.ds(*GATHER[0])):
            acc[low, cols] = new

        for c in range(1, len(GATHER)):
            landing = recvs[c - 1]
            others = landing.at[pl.ds(0, DP - 1)]
            pltpu.make_async_copy(others, others, lead_recv.at[c - 1]).wait()

            def unpack_lead(j, total, landing=landing, start=GATHER[c][0]):
                return unpack(landing[2 * j].astype(F32), landing[2 * j + 1].astype(F32), j, start, total)

            squared = lax.fori_loop(0, DP // 2, unpack_lead, squared, unroll=4)
            for low, cols, new in grams(pl.ds(*GATHER[c])):
                acc[low, cols] += new

        norm = jnp.sqrt(jnp.sum(squared, axis=(0, 1), keepdims=True)) + epsilon
        inverse = 1.0 / norm

        def put(ref, n, value):
            value = value.astype(BF16)
            low, cols = lower(n)
            ref[low, cols] = value
            for m in range(n + 1, 3):
                ref[cols, pl.ds(256 * m, 256)] = value[256 * (m - n) : 256 * (m - n) + 256].T

        def product(left, right, n):
            low, cols = lower(n)
            return jnp.dot(left[low, :], right[:, cols], preferred_element_type=F32)

        def block(ref, n):
            return ref[lower(n)].astype(F32)

        for n in range(3):
            put(gram, n, acc[lower(n)] * inverse * inverse)
        for n in range(3):
            put(mix, n, cub_coef * block(gram, n) + quint_coef * product(gram, gram, n))
        for n in range(3):
            new = product(mix, gram, n)
            put(prod, n, new)
            acc[lower(n)] = lin_coef * lin_coef * block(gram, n) + 2.0 * lin_coef * new
        for n in range(3):
            put(gram, n, acc[lower(n)] + product(mix, prod, n))
        for n in range(3):
            put(mix2, n, cub_coef * block(gram, n) + quint_coef * product(gram, gram, n))
        for n in range(3):
            put(prod, n, lin_coef * (block(mix, n) + block(mix2, n)) + product(mix2, mix, n))

        scale = inverse * (0.2 * math.sqrt(max(FULL, WIDTH)))

        for c, (start, width) in enumerate(SPREAD):
            half = width // 2
            parts = []
            for columns in (pl.ds(start, half), pl.ds(start + half, half)):
                right = full[:, columns]
                new = jnp.dot(prod[...], right, preferred_element_type=F32)
                parts.append((new + lin_coef * lin_coef * right.astype(F32)) * scale)
            for d in range(DP):
                rows = slice(d * ROWS, (d + 1) * ROWS)
                outgoing[c][d] = jnp.concatenate([part[rows] for part in parts], axis=0).astype(BF16)

            returned[c][my_k] = outgoing[c][me]

            def send(i, carry, c=c):
                dest = lax.rem(me + i, DP)
                pltpu.make_async_remote_copy(
                    src_ref=outgoing[c].at[dest], dst_ref=returned[c].at[my_k], send_sem=ret_send.at[c],
                    recv_sem=ret_recv.at[c], device_id=(z, dest), device_id_type=MESH,
                ).start()
                return carry

            lax.fori_loop(1, DP, send, 0)

    stores = []
    for c, (start, width) in enumerate(SPREAD):
        landing = returned[c]

        @pl.when(is_owner)
        def _():
            others = landing.at[pl.ds(0, MATS - 1)]
            pltpu.make_async_copy(others, others, ret_recv.at[c]).wait()

        @pl.when(jnp.logical_not(is_owner))
        def _():
            pltpu.make_async_copy(landing, landing, ret_recv.at[c]).wait()

        def unpack_result(k, carry, landing=landing, start=start, half=width // 2):
            piece = landing[k].astype(F32)
            up_v[k, :, pl.ds(start, half)] = piece[:ROWS].astype(BF16)
            up_v[k, :, pl.ds(start + half, half)] = piece[ROWS:].astype(BF16)
            return carry

        lax.fori_loop(0, MATS, unpack_result, 0, unroll=4)
        columns = pl.ds(start, width)
        stores.append(pltpu.make_async_copy(up_v.at[:, :, columns], up_hbm.at[:, :, columns], out_sem.at[1 + c]))
        stores[-1].start()

    for stage, part in ((0, part_a), (1, part_b)):
        others = part.at[pl.ds(0, SUM_PEERS - 1)]
        pltpu.make_async_copy(others, others, sum_send.at[stage]).wait()

    @pl.when(is_owner)
    def _():
        others = raw.at[pl.ds(0, 2 * (MATS - 1))]
        pltpu.make_async_copy(others, others, raw_send).wait()
        for c, buffer in enumerate(leads):
            others = buffer.at[pl.ds(0, MATS - 1)]
            pltpu.make_async_copy(others, others, lead_send.at[c]).wait()
        for c, buffer in enumerate(outgoing):
            others = buffer.at[pl.ds(0, DP - 1)]
            pltpu.make_async_copy(others, others, ret_send.at[c]).wait()

    @pl.when(jnp.logical_not(is_owner))
    def _():
        pltpu.make_async_copy(raw, raw, raw_send).wait()
        for c, buffer in enumerate(leads):
            pltpu.make_async_copy(buffer, buffer, lead_send.at[c]).wait()

    store_nm.wait()
    for store in stores:
        store.wait()


def shards(grads, momentum):
    shape = grads.shape
    flat = (MATS, ROWS, WIDTH)
    out = jax.ShapeDtypeStruct(flat, BF16)
    square = (FULL, FULL)
    new_momentum, update = pl.pallas_call(
        kernel,
        out_shape=(out, out),
        in_specs=[pl.BlockSpec(memory_space=pl.ANY)] * 2,
        out_specs=(pl.BlockSpec(memory_space=pl.ANY),) * 2,
        scratch_shapes=[
            pltpu.VMEM(flat, BF16),
            pltpu.VMEM(flat, BF16),
            pltpu.VMEM(flat, BF16),
            pltpu.VMEM(flat, BF16),
            pieces(2 * MATS, NARROW),
            pieces(DP, NARROW),
            pieces(DP, NARROW),
            [pieces(MATS, width) for _, width in GATHER[1:]],
            [pieces(DP, width) for _, width in GATHER[1:]],
            pltpu.VMEM((FULL, WIDTH), BF16),
            pltpu.VMEM(square, F32),
            pltpu.VMEM(square, BF16),
            pltpu.VMEM(square, BF16),
            pltpu.VMEM(square, BF16),
            pltpu.VMEM(square, BF16),
            [pieces(DP, width) for _, width in SPREAD],
            [pieces(MATS, width) for _, width in SPREAD],
            pltpu.VMEM((SUM_PEERS, 8, 128), F32),
            pltpu.VMEM((SUM_PEERS, 8, 128), F32),
            pltpu.SemaphoreType.DMA((4,)),
            pltpu.SemaphoreType.DMA,
            pltpu.SemaphoreType.DMA((1 + len(SPREAD),)),
            pltpu.SemaphoreType.DMA((2,)),
            pltpu.SemaphoreType.DMA((2,)),
            pltpu.SemaphoreType.DMA,
            pltpu.SemaphoreType.DMA((2,)),
            pltpu.SemaphoreType.DMA((len(GATHER) - 1,)),
            pltpu.SemaphoreType.DMA((len(GATHER) - 1,)),
            pltpu.SemaphoreType.DMA((len(SPREAD),)),
            pltpu.SemaphoreType.DMA((len(SPREAD),)),
        ],
        compiler_params=pltpu.CompilerParams(
            collective_id=0, has_side_effects=True, vmem_limit_bytes=51 * 1024 * 1024 + 256 * 1024
        ),
        name="muon_step",
    )(grads.reshape(flat), momentum.reshape(flat))
    return new_momentum.reshape(shape), update.reshape(shape)


def solution(mesh):
    placed = (P("expert", None, "dp", None), P("expert", None, "dp", None))
    return jax.shard_map(
        shards,
        mesh=mesh,
        in_specs=placed,
        out_specs=(P("expert", None, "dp", None), P("expert", None, "dp", None)),
        check_vma=False,
    )
```

```python
import functools
import math

import jax
import jax.numpy as jnp
from jax import lax
from jax.experimental import pallas as pl
from jax.experimental.pallas import tpu as pltpu
from jax.sharding import PartitionSpec as P

lin_coef = 3.4445
cub_coef = -4.775
quint_coef = 2.0315
epsilon = 1e-07
momentum_rate = 0.95

MESH = pl.DeviceIdType.MESH
F32 = jnp.float32
BF16 = jnp.bfloat16

SIDE = 4
CHIPS = SIDE * SIDE
PLANES = 8
DP = 2 * CHIPS
MATS = 12
ROWS = 24
WIDTH = 2048
FULL = ROWS * DP
COLS = 512
NARROW = 256
PIECE = 2 * ROWS
SUM_PEERS = 16
GATHER = ((0, NARROW), (NARROW, NARROW), (512, COLS), (1024, COLS), (1536, COLS))
SPREAD = ((0, NARROW), (512, COLS), (1024, COLS), (1536, COLS), (NARROW, NARROW))


def hops(step, size):
    return min(step, size - step)


FAR_A = sorted(
    ((dz, other) for dz in range(PLANES) for other in range(2) if dz or other), key=lambda p: -hops(p[0], PLANES)
)
FAR_B = sorted(
    ((dy, dx) for dy in range(SIDE) for dx in range(SIDE) if dy or dx),
    key=lambda p: -hops(p[0], SIDE) - hops(p[1], SIDE),
)


def owner_of(k, z):
    x = k // (SIDE - 1)
    y = lax.rem(x + z + 1 + lax.rem(k, SIDE - 1), SIDE)
    return (y * SIDE + x) * 2


def shifted(z, t, core, sign):
    step = jnp.where(t == 1, 1, jnp.where(t == 2, 2 - 4 * core, -1))
    return lax.rem(z + PLANES + sign * step, PLANES)


def stack_halves(wide):
    half = wide.shape[1] // 2
    return jnp.concatenate([wide[:, :half], wide[:, half:]], axis=0)


def pieces(count, columns):
    return pltpu.VMEM((count, PIECE, columns // 2), BF16)


def kernel(
    g_hbm, m_hbm, nm_hbm, up_hbm,
    g_v, m_v, nm_v, up_v, raw, recv_g, recv_m, leads, recvs, full, acc, gram, mix, prod, mix2, outgoing, returned, passing, bouncing, part_a, part_b,
    g_sem, m_sem, out_sem, sum_send, sum_recv, raw_send, raw_recv, lead_send, lead_recv, ret_send, ret_recv, pass_send, pass_recv, bounce_send, bounce_recv,
):
    z = lax.axis_index("expert")
    me = lax.axis_index("dp")
    chip = me // 2
    core = lax.rem(me, 2)
    my_y = chip // SIDE
    my_x = lax.rem(chip, SIDE)
    my_t = lax.rem(my_y - my_x - z + 3 * SIDE, SIDE)
    is_owner = jnp.logical_and(core == 0, my_t != 0)
    my_k = my_x * (SIDE - 1) + my_t - 1

    line = z * 2 + core

    def peer_a(i):
        dz, other = FAR_A[i - 1]
        return (lax.rem(z + dz, PLANES), chip * 2 + (1 - core if other else core))

    def peer_b(i):
        dy, dx = FAR_B[i - 1]
        return (z, (lax.rem(my_y + dy, SIDE) * SIDE + lax.rem(my_x + dx, SIDE)) * 2 + core)

    for k in range(4):
        part = pl.ds(3 * k, 3)
        pltpu.make_async_copy(g_hbm.at[part], g_v.at[part], g_sem.at[k]).start()
    load_m = pltpu.make_async_copy(m_hbm, m_v, m_sem)
    load_m.start()

    barrier = pltpu.get_barrier_semaphore()
    for i in range(1, SUM_PEERS):
        pl.semaphore_signal(barrier, inc=1, device_id=peer_a(i), device_id_type=MESH)
        pl.semaphore_signal(barrier, inc=1, device_id=peer_b(i), device_id_type=MESH)

    @pl.when(is_owner)
    def _():
        for i in range(1, CHIPS):
            other = (z, lax.rem(chip + i, CHIPS) * 2 + 1)
            pl.semaphore_signal(barrier, inc=1, device_id=other, device_id_type=MESH)

    total = jnp.zeros((8, 128), F32)
    for k in range(4):
        part = pl.ds(3 * k, 3)
        pltpu.make_async_copy(g_hbm.at[part], g_v.at[part], g_sem.at[k]).wait()

        def squares(i, carry):
            wide = g_v[i // 4, :, pl.ds(pl.multiple_of(lax.rem(i, 4) * COLS, COLS), COLS)].astype(F32)
            wide = wide * wide
            wide = wide[0:8] + wide[8:16] + wide[16:24]
            wide = wide[:, 0:256] + wide[:, 256:512]
            return carry + (wide[:, 0:128] + wide[:, 128:256])

        total = lax.fori_loop(12 * k, 12 * k + 12, squares, total, unroll=4)

    others_owning = jnp.where(my_t != 0, MATS - 1, MATS)
    pl.semaphore_wait(barrier, 2 * (SUM_PEERS - 1) + jnp.where(core == 1, others_owning, 0))

    def send_sum(total, part, slot, peer, stage):
        part[slot] = total
        for i in range(1, SUM_PEERS):
            pltpu.make_async_remote_copy(
                src_ref=part.at[slot], dst_ref=part.at[slot], send_sem=sum_send.at[stage], recv_sem=sum_recv.at[stage],
                device_id=peer(i), device_id_type=MESH,
            ).start()

    def take_sum(part, stage):
        others = part.at[pl.ds(0, SUM_PEERS - 1)]
        pltpu.make_async_copy(others, others, sum_recv.at[stage]).wait()
        return jnp.sum(part[...], axis=0)

    def push(piece, buffer, slot, landing, k, send_sem, recv_sem):
        dest = owner_of(k, z)
        buffer[slot] = piece

        @pl.when(dest == me)
        def _():
            landing[me] = piece

        @pl.when(dest != me)
        def _():
            pltpu.make_async_remote_copy(
                src_ref=buffer.at[slot], dst_ref=landing.at[me], send_sem=send_sem, recv_sem=recv_sem,
                device_id=(z, dest), device_id_type=MESH,
            ).start()

    send_sum(total, part_a, line, peer_a, 0)
    load_m.wait()

    def send_raw(i, carry):
        k = lax.rem(i + me, MATS)
        push(stack_halves(g_v[k, :, :NARROW].astype(F32)).astype(BF16), raw, k, recv_g, k, raw_send, raw_recv.at[0])
        push(stack_halves(m_v[k, :, :NARROW].astype(F32)).astype(BF16), raw, MATS + k, recv_m, k, raw_send, raw_recv.at[1])
        return carry

    lax.fori_loop(0, MATS, send_raw, 0)
    total = take_sum(part_a, 0)
    send_sum(total, part_b, chip, peer_b, 1)
    total = take_sum(part_b, 1)
    count = MATS * PLANES * FULL * WIDTH
    mean = jnp.sum(total, axis=(0, 1), keepdims=True) / count
    clip = 1.0 / jnp.maximum(jnp.sqrt(mean), 1.0)

    def combine(g, m):
        scaled = clip * g.astype(F32)
        moment = momentum_rate * m.astype(F32) + scaled
        return moment, scaled + momentum_rate * moment

    def send_around(i, carry):
        k = lax.rem(i + me, MATS)
        t = lax.rem(k, SIDE - 1) + 1
        columns = pl.ds(*GATHER[1])
        leads[0][k] = stack_halves(combine(g_v[k, :, columns], m_v[k, :, columns])[1]).astype(BF16)
        pltpu.make_async_remote_copy(
            src_ref=leads[0].at[k], dst_ref=passing.at[t - 1, chip], send_sem=lead_send.at[0],
            recv_sem=pass_recv.at[t - 1], device_id=(shifted(z, t, core, 1), owner_of(k, z) + core), device_id_type=MESH,
        ).start()
        return carry

    lax.fori_loop(0, MATS, send_around, 0)

    for c in range(2, len(GATHER)):
        columns = pl.ds(*GATHER[c])

        def send_lead(i, carry, columns=columns, c=c):
            k = lax.rem(i + me, MATS)
            piece = stack_halves(combine(g_v[k, :, columns], m_v[k, :, columns])[1]).astype(BF16)
            push(piece, leads[c - 1], k, recvs[c - 1], k, lead_send.at[c - 1], lead_recv.at[c - 1])
            return carry

        lax.fori_loop(0, MATS, send_lead, 0)

    @pl.when(my_t == 0)
    def _():
        for t in (2, 1, 3):
            every = passing.at[t - 1]
            pltpu.make_async_copy(every, every, pass_recv.at[t - 1]).wait()

            def hand_on(i, carry, t=t):
                source = lax.rem(i + chip, CHIPS)
                pltpu.make_async_remote_copy(
                    src_ref=passing.at[t - 1, source], dst_ref=recvs[0].at[source * 2 + core], send_sem=pass_send,
                    recv_sem=lead_recv.at[0], device_id=(shifted(z, t, core, -1), chip * 2), device_id_type=MESH,
                ).start()
                return carry

            lax.fori_loop(0, CHIPS, hand_on, 0)

    def momentum_step(i, carry):
        k = i // 4
        columns = pl.ds(pl.multiple_of(lax.rem(i, 4) * COLS, COLS), COLS)
        nm_v[k, :, columns] = combine(g_v[k, :, columns], m_v[k, :, columns])[0].astype(BF16)
        return carry

    lax.fori_loop(0, 4 * MATS, momentum_step, 0, unroll=4)
    store_nm = pltpu.make_async_copy(nm_v, nm_hbm, out_sem.at[0])
    store_nm.start()

    @pl.when(is_owner)
    def _():
        def unpack(one, two, j, start, total):
            half = one.shape[1]
            rows = pl.ds(pl.multiple_of(j * PIECE, PIECE), PIECE)
            full[rows, pl.ds(start, half)] = jnp.concatenate([one[:ROWS], two[:ROWS]], axis=0).astype(BF16)
            full[rows, pl.ds(start + half, half)] = jnp.concatenate([one[ROWS:], two[ROWS:]], axis=0).astype(BF16)
            both = one * one + two * two
            if half == 256:
                both = both[:, :128] + both[:, 128:]
            return total + (both[0:8] + both[8:16] + both[16:24] + both[24:32] + both[32:40] + both[40:48])

        def lower(n):
            return pl.ds(256 * n, FULL - 256 * n), pl.ds(256 * n, 256)

        def grams(columns):
            for n in range(3):
                low, cols = lower(n)
                new = lax.dot_general(
                    full[low, columns], full[cols, columns], (((1,), (1,)), ((), ())), preferred_element_type=F32
                )
                yield low, cols, new

        for stage, landing in ((0, recv_g), (1, recv_m)):
            others = landing.at[pl.ds(0, DP - 1)]
            pltpu.make_async_copy(others, others, raw_recv.at[stage]).wait()

        def unpack_raw(j, total):
            one = combine(recv_g[2 * j], recv_m[2 * j])[1].astype(BF16).astype(F32)
            two = combine(recv_g[2 * j + 1], recv_m[2 * j + 1])[1].astype(BF16).astype(F32)
            return unpack(one, two, j, 0, total)

        squared = lax.fori_loop(0, DP // 2, unpack_raw, jnp.zeros((8, 128), F32), unroll=4)
        for low, cols, new in grams(pl.ds(*GATHER[0])):
            acc[low, cols] = new

        for c in (*range(2, len(GATHER)), 1):
            landing = recvs[c - 1]
            arriving = landing.at[pl.ds(0, DP if c == 1 else DP - 1)]
            pltpu.make_async_copy(arriving, arriving, lead_recv.at[c - 1]).wait()

            def unpack_lead(j, total, landing=landing, start=GATHER[c][0]):
                return unpack(landing[2 * j].astype(F32), landing[2 * j + 1].astype(F32), j, start, total)

            squared = lax.fori_loop(0, DP // 2, unpack_lead, squared, unroll=4)
            for low, cols, new in grams(pl.ds(*GATHER[c])):
                acc[low, cols] += new

        norm = jnp.sqrt(jnp.sum(squared, axis=(0, 1), keepdims=True)) + epsilon
        inverse = 1.0 / norm

        def put(ref, n, value):
            value = value.astype(BF16)
            low, cols = lower(n)
            ref[low, cols] = value
            for m in range(n + 1, 3):
                ref[cols, pl.ds(256 * m, 256)] = value[256 * (m - n) : 256 * (m - n) + 256].T

        def product(left, right, n):
            low, cols = lower(n)
            return jnp.dot(left[low, :], right[:, cols], preferred_element_type=F32)

        def block(ref, n):
            return ref[lower(n)].astype(F32)

        for n in range(3):
            put(gram, n, acc[lower(n)] * inverse * inverse)
        for n in range(3):
            put(mix, n, cub_coef * block(gram, n) + quint_coef * product(gram, gram, n))
        for n in range(3):
            new = product(mix, gram, n)
            put(prod, n, new)
            acc[lower(n)] = lin_coef * lin_coef * block(gram, n) + 2.0 * lin_coef * new
        for n in range(3):
            put(gram, n, acc[lower(n)] + product(mix, prod, n))
        for n in range(3):
            put(mix2, n, cub_coef * block(gram, n) + quint_coef * product(gram, gram, n))
        for n in range(3):
            put(prod, n, lin_coef * (block(mix, n) + block(mix2, n)) + product(mix2, mix, n))

        scale = inverse * (0.2 * math.sqrt(max(FULL, WIDTH)))

        for c, (start, width) in enumerate(SPREAD):
            half = width // 2
            parts = []
            for columns in (pl.ds(start, half), pl.ds(start + half, half)):
                right = full[:, columns]
                new = jnp.dot(prod[...], right, preferred_element_type=F32)
                parts.append((new + lin_coef * lin_coef * right.astype(F32)) * scale)
            for d in range(DP):
                rows = slice(d * ROWS, (d + 1) * ROWS)
                outgoing[c][d] = jnp.concatenate([part[rows] for part in parts], axis=0).astype(BF16)

            if c > 0:
                returned[c][my_k] = outgoing[c][me]

            def send(i, carry, c=c):
                dest = lax.rem(me + i, DP)
                if c == 0:
                    landing, sem = bouncing.at[(my_t - 1) * SIDE + my_x], bounce_recv
                else:
                    landing, sem = returned[c].at[my_k], ret_recv.at[c]
                pltpu.make_async_remote_copy(
                    src_ref=outgoing[c].at[dest], dst_ref=landing, send_sem=ret_send.at[c], recv_sem=sem,
                    device_id=(shifted(z, my_t, lax.rem(dest, 2), 1) if c == 0 else z, dest), device_id_type=MESH,
                ).start()
                return carry

            lax.fori_loop(0 if c == 0 else 1, DP, send, 0)

    pltpu.make_async_copy(bouncing, bouncing, bounce_recv).wait()

    def bounce(i, carry):
        t = i // SIDE + 1
        pltpu.make_async_remote_copy(
            src_ref=bouncing.at[i], dst_ref=returned[0].at[lax.rem(i, SIDE) * (SIDE - 1) + t - 1], send_sem=bounce_send,
            recv_sem=ret_recv.at[0], device_id=(shifted(z, t, core, -1), me), device_id_type=MESH,
        ).start()
        return carry

    lax.fori_loop(0, MATS, bounce, 0)

    stores = []
    for c in (*range(1, len(SPREAD)), 0):
        start, width = SPREAD[c]
        landing = returned[c]

        if c == 0:
            pltpu.make_async_copy(landing, landing, ret_recv.at[c]).wait()
        else:

            @pl.when(is_owner)
            def _():
                others = landing.at[pl.ds(0, MATS - 1)]
                pltpu.make_async_copy(others, others, ret_recv.at[c]).wait()

            @pl.when(jnp.logical_not(is_owner))
            def _():
                pltpu.make_async_copy(landing, landing, ret_recv.at[c]).wait()

        def unpack_result(k, carry, landing=landing, start=start, half=width // 2):
            piece = landing[k].astype(F32)
            up_v[k, :, pl.ds(start, half)] = piece[:ROWS].astype(BF16)
            up_v[k, :, pl.ds(start + half, half)] = piece[ROWS:].astype(BF16)
            return carry

        lax.fori_loop(0, MATS, unpack_result, 0, unroll=4)
        columns = pl.ds(start, width)
        stores.append(pltpu.make_async_copy(up_v.at[:, :, columns], up_hbm.at[:, :, columns], out_sem.at[1 + c]))
        stores[-1].start()

    for stage, part in ((0, part_a), (1, part_b)):
        others = part.at[pl.ds(0, SUM_PEERS - 1)]
        pltpu.make_async_copy(others, others, sum_send.at[stage]).wait()

    @pl.when(is_owner)
    def _():
        others = raw.at[pl.ds(0, 2 * (MATS - 1))]
        pltpu.make_async_copy(others, others, raw_send).wait()
        for c, buffer in enumerate(leads):
            sent = buffer.at[pl.ds(0, MATS if c == 0 else MATS - 1)]
            pltpu.make_async_copy(sent, sent, lead_send.at[c]).wait()
        for c, buffer in enumerate(outgoing):
            sent = buffer.at[pl.ds(0, DP if c == 0 else DP - 1)]
            pltpu.make_async_copy(sent, sent, ret_send.at[c]).wait()

    @pl.when(jnp.logical_not(is_owner))
    def _():
        pltpu.make_async_copy(raw, raw, raw_send).wait()
        for c, buffer in enumerate(leads):
            pltpu.make_async_copy(buffer, buffer, lead_send.at[c]).wait()

    @pl.when(my_t == 0)
    def _():
        pltpu.make_async_copy(passing, passing, pass_send).wait()

    pltpu.make_async_copy(bouncing, bouncing, bounce_send).wait()
    store_nm.wait()
    for store in stores:
        store.wait()


def shards(grads, momentum):
    shape = grads.shape
    flat = (MATS, ROWS, WIDTH)
    out = jax.ShapeDtypeStruct(flat, BF16)
    square = (FULL, FULL)
    new_momentum, update = pl.pallas_call(
        kernel,
        out_shape=(out, out),
        in_specs=[pl.BlockSpec(memory_space=pl.ANY)] * 2,
        out_specs=(pl.BlockSpec(memory_space=pl.ANY),) * 2,
        scratch_shapes=[
            pltpu.VMEM(flat, BF16),
            pltpu.VMEM(flat, BF16),
            pltpu.VMEM(flat, BF16),
            pltpu.VMEM(flat, BF16),
            pieces(2 * MATS, NARROW),
            pieces(DP, NARROW),
            pieces(DP, NARROW),
            [pieces(MATS, width) for _, width in GATHER[1:]],
            [pieces(DP, width) for _, width in GATHER[1:]],
            pltpu.VMEM((FULL, WIDTH), BF16),
            pltpu.VMEM(square, F32),
            pltpu.VMEM(square, BF16),
            pltpu.VMEM(square, BF16),
            pltpu.VMEM(square, BF16),
            pltpu.VMEM(square, BF16),
            [pieces(DP, width) for _, width in SPREAD],
            [pieces(MATS, width) for _, width in SPREAD],
            pltpu.VMEM((SIDE - 1, CHIPS, PIECE, NARROW // 2), BF16),
            pieces(MATS, NARROW),
            pltpu.VMEM((SUM_PEERS, 8, 128), F32),
            pltpu.VMEM((SUM_PEERS, 8, 128), F32),
            pltpu.SemaphoreType.DMA((4,)),
            pltpu.SemaphoreType.DMA,
            pltpu.SemaphoreType.DMA((1 + len(SPREAD),)),
            pltpu.SemaphoreType.DMA((2,)),
            pltpu.SemaphoreType.DMA((2,)),
            pltpu.SemaphoreType.DMA,
            pltpu.SemaphoreType.DMA((2,)),
            pltpu.SemaphoreType.DMA((len(GATHER) - 1,)),
            pltpu.SemaphoreType.DMA((len(GATHER) - 1,)),
            pltpu.SemaphoreType.DMA((len(SPREAD),)),
            pltpu.SemaphoreType.DMA((len(SPREAD),)),
            pltpu.SemaphoreType.DMA,
            pltpu.SemaphoreType.DMA((SIDE - 1,)),
            pltpu.SemaphoreType.DMA,
            pltpu.SemaphoreType.DMA,
        ],
        compiler_params=pltpu.CompilerParams(
            collective_id=0, has_side_effects=True, vmem_limit_bytes=51 * 1024 * 1024 + 256 * 1024
        ),
        name="muon_step",
    )(grads.reshape(flat), momentum.reshape(flat))
    return new_momentum.reshape(shape), update.reshape(shape)


def solution(mesh):
    placed = (P("expert", None, "dp", None), P("expert", None, "dp", None))
    return jax.shard_map(
        shards,
        mesh=mesh,
        in_specs=placed,
        out_specs=(P("expert", None, "dp", None), P("expert", None, "dp", None)),
        check_vma=False,
    )
```

```python
import functools
import math

import jax
import jax.numpy as jnp
from jax import lax
from jax.experimental import pallas as pl
from jax.experimental.pallas import tpu as pltpu
from jax.sharding import PartitionSpec as P

lin_coef = 3.4445
cub_coef = -4.775
quint_coef = 2.0315
epsilon = 1e-07
momentum_rate = 0.95

MESH = pl.DeviceIdType.MESH
F32 = jnp.float32
BF16 = jnp.bfloat16

SIDE = 4
CHIPS = SIDE * SIDE
PLANES = 8
DP = 2 * CHIPS
MATS = 12
ROWS = 24
WIDTH = 2048
FULL = ROWS * DP
COLS = 512
NARROW = 256
PIECE = 2 * ROWS
SUM_PEERS = 16
GATHER = ((0, NARROW), (NARROW, NARROW), (512, COLS), (1024, COLS), (1536, COLS))
SPREAD = ((0, NARROW), (NARROW, NARROW), (512, COLS), (1024, COLS), (1536, COLS))
AROUND = 1


def hops(step, size):
    return min(step, size - step)


FAR_A = sorted(
    ((dz, other) for dz in range(PLANES) for other in range(2) if dz or other), key=lambda p: -hops(p[0], PLANES)
)
FAR_B = sorted(
    ((dy, dx) for dy in range(SIDE) for dx in range(SIDE) if dy or dx),
    key=lambda p: -hops(p[0], SIDE) - hops(p[1], SIDE),
)


def owner_of(k, z):
    x = k // (SIDE - 1)
    y = lax.rem(x + z + 1 + lax.rem(k, SIDE - 1), SIDE)
    return (y * SIDE + x) * 2


def shifted(z, t, core, sign):
    step = jnp.where(t == 1, 1, jnp.where(t == 2, 2 - 4 * core, -1))
    return lax.rem(z + PLANES + sign * step, PLANES)


def stack_halves(wide):
    half = wide.shape[1] // 2
    return jnp.concatenate([wide[:, :half], wide[:, half:]], axis=0)


def pieces(count, columns):
    return pltpu.VMEM((count, PIECE, columns // 2), BF16)


def kernel(
    g_hbm, m_hbm, nm_hbm, up_hbm,
    g_v, m_v, nm_v, up_v, raw, recv_g, recv_m, leads, recvs, full, acc, gram, mix, prod, mix2, outgoing, returned, passing, bouncing, part_a, part_b,
    g_sem, m_sem, out_sem, sum_send, sum_recv, raw_send, raw_recv, lead_send, lead_recv, ret_send, ret_recv, pass_send, pass_recv, bounce_send, bounce_recv,
):
    z = lax.axis_index("expert")
    me = lax.axis_index("dp")
    chip = me // 2
    core = lax.rem(me, 2)
    my_y = chip // SIDE
    my_x = lax.rem(chip, SIDE)
    my_t = lax.rem(my_y - my_x - z + 3 * SIDE, SIDE)
    is_owner = jnp.logical_and(core == 0, my_t != 0)
    my_k = my_x * (SIDE - 1) + my_t - 1

    line = z * 2 + core

    def peer_a(i):
        dz, other = FAR_A[i - 1]
        return (lax.rem(z + dz, PLANES), chip * 2 + (1 - core if other else core))

    def peer_b(i):
        dy, dx = FAR_B[i - 1]
        return (z, (lax.rem(my_y + dy, SIDE) * SIDE + lax.rem(my_x + dx, SIDE)) * 2 + core)

    for k in range(4):
        part = pl.ds(3 * k, 3)
        pltpu.make_async_copy(g_hbm.at[part], g_v.at[part], g_sem.at[k]).start()
    load_m = pltpu.make_async_copy(m_hbm, m_v, m_sem)

    barrier = pltpu.get_barrier_semaphore()
    for i in range(1, SUM_PEERS):
        pl.semaphore_signal(barrier, inc=1, device_id=peer_a(i), device_id_type=MESH)
        pl.semaphore_signal(barrier, inc=1, device_id=peer_b(i), device_id_type=MESH)

    @pl.when(is_owner)
    def _():
        for i in range(1, CHIPS):
            other = (z, lax.rem(chip + i, CHIPS) * 2 + 1)
            pl.semaphore_signal(barrier, inc=1, device_id=other, device_id_type=MESH)

    total = jnp.zeros((8, 128), F32)
    for k in range(4):
        part = pl.ds(3 * k, 3)
        pltpu.make_async_copy(g_hbm.at[part], g_v.at[part], g_sem.at[k]).wait()

        def squares(i, carry):
            wide = g_v[i // 4, :, pl.ds(pl.multiple_of(lax.rem(i, 4) * COLS, COLS), COLS)].astype(F32)
            wide = wide * wide
            wide = wide[0:8] + wide[8:16] + wide[16:24]
            wide = wide[:, 0:256] + wide[:, 256:512]
            return carry + (wide[:, 0:128] + wide[:, 128:256])

        if k == 3:
            load_m.start()
        total = lax.fori_loop(12 * k, 12 * k + 12, squares, total, unroll=4)

    others_owning = jnp.where(my_t != 0, MATS - 1, MATS)
    pl.semaphore_wait(barrier, 2 * (SUM_PEERS - 1) + jnp.where(core == 1, others_owning, 0))

    def send_sum(total, part, slot, peer, stage):
        part[slot] = total
        for i in range(1, SUM_PEERS):
            pltpu.make_async_remote_copy(
                src_ref=part.at[slot], dst_ref=part.at[slot], send_sem=sum_send.at[stage], recv_sem=sum_recv.at[stage],
                device_id=peer(i), device_id_type=MESH,
            ).start()

    def take_sum(part, stage):
        others = part.at[pl.ds(0, SUM_PEERS - 1)]
        pltpu.make_async_copy(others, others, sum_recv.at[stage]).wait()
        return jnp.sum(part[...], axis=0)

    def push(piece, buffer, slot, landing, k, send_sem, recv_sem):
        dest = owner_of(k, z)
        buffer[slot] = piece

        @pl.when(dest == me)
        def _():
            landing[me] = piece

        @pl.when(dest != me)
        def _():
            pltpu.make_async_remote_copy(
                src_ref=buffer.at[slot], dst_ref=landing.at[me], send_sem=send_sem, recv_sem=recv_sem,
                device_id=(z, dest), device_id_type=MESH,
            ).start()

    send_sum(total, part_a, line, peer_a, 0)
    load_m.wait()

    def send_raw(i, carry):
        k = lax.rem(i + me, MATS)
        push(stack_halves(g_v[k, :, :NARROW].astype(F32)).astype(BF16), raw, k, recv_g, k, raw_send, raw_recv.at[0])
        push(stack_halves(m_v[k, :, :NARROW].astype(F32)).astype(BF16), raw, MATS + k, recv_m, k, raw_send, raw_recv.at[1])
        return carry

    lax.fori_loop(0, MATS, send_raw, 0)
    total = take_sum(part_a, 0)
    send_sum(total, part_b, chip, peer_b, 1)
    total = take_sum(part_b, 1)
    count = MATS * PLANES * FULL * WIDTH
    mean = jnp.sum(total, axis=(0, 1), keepdims=True) / count
    clip = 1.0 / jnp.maximum(jnp.sqrt(mean), 1.0)

    def combine(g, m):
        scaled = clip * g.astype(F32)
        moment = momentum_rate * m.astype(F32) + scaled
        return moment, scaled + momentum_rate * moment

    def send_around(i, carry):
        k = lax.rem(i + me, MATS)
        t = lax.rem(k, SIDE - 1) + 1
        columns = pl.ds(*GATHER[1])
        leads[0][k] = stack_halves(combine(g_v[k, :, columns], m_v[k, :, columns])[1]).astype(BF16)
        pltpu.make_async_remote_copy(
            src_ref=leads[0].at[k], dst_ref=passing.at[t - 1, chip], send_sem=lead_send.at[0],
            recv_sem=pass_recv.at[t - 1], device_id=(shifted(z, t, core, 1), owner_of(k, z) + core), device_id_type=MESH,
        ).start()
        return carry

    for c in range(2, len(GATHER)):
        columns = pl.ds(*GATHER[c])

        def send_lead(i, carry, columns=columns, c=c):
            if c == 2:
                send_around(i, carry)
            k = lax.rem(i + me, MATS)
            piece = stack_halves(combine(g_v[k, :, columns], m_v[k, :, columns])[1]).astype(BF16)
            push(piece, leads[c - 1], k, recvs[c - 1], k, lead_send.at[c - 1], lead_recv.at[c - 1])
            return carry

        lax.fori_loop(0, MATS, send_lead, 0, unroll=2)

    @pl.when(my_t == 0)
    def _():
        for t in (2, 1, 3):
            every = passing.at[t - 1]
            pltpu.make_async_copy(every, every, pass_recv.at[t - 1]).wait()

            def hand_on(i, carry, t=t):
                source = lax.rem(i + chip, CHIPS)
                pltpu.make_async_remote_copy(
                    src_ref=passing.at[t - 1, source], dst_ref=recvs[0].at[source * 2 + core], send_sem=pass_send,
                    recv_sem=lead_recv.at[0], device_id=(shifted(z, t, core, -1), chip * 2), device_id_type=MESH,
                ).start()
                return carry

            lax.fori_loop(0, CHIPS, hand_on, 0)

    def momentum_step(i, carry):
        k = i // 4
        columns = pl.ds(pl.multiple_of(lax.rem(i, 4) * COLS, COLS), COLS)
        nm_v[k, :, columns] = combine(g_v[k, :, columns], m_v[k, :, columns])[0].astype(BF16)
        return carry

    lax.fori_loop(0, 4 * MATS, momentum_step, 0, unroll=4)
    store_nm = pltpu.make_async_copy(nm_v, nm_hbm, out_sem.at[0])
    store_nm.start()

    @pl.when(is_owner)
    def _():
        def unpack(one, two, j, start, total):
            half = one.shape[1]
            rows = pl.ds(pl.multiple_of(j * PIECE, PIECE), PIECE)
            full[rows, pl.ds(start, half)] = jnp.concatenate([one[:ROWS], two[:ROWS]], axis=0).astype(BF16)
            full[rows, pl.ds(start + half, half)] = jnp.concatenate([one[ROWS:], two[ROWS:]], axis=0).astype(BF16)
            both = one * one + two * two
            if half == 256:
                both = both[:, :128] + both[:, 128:]
            return total + (both[0:8] + both[8:16] + both[16:24] + both[24:32] + both[32:40] + both[40:48])

        def lower(n):
            return pl.ds(256 * n, FULL - 256 * n), pl.ds(256 * n, 256)

        def grams(columns):
            for n in range(3):
                low, cols = lower(n)
                new = lax.dot_general(
                    full[low, columns], full[cols, columns], (((1,), (1,)), ((), ())), preferred_element_type=F32
                )
                yield low, cols, new

        for stage, landing in ((0, recv_g), (1, recv_m)):
            others = landing.at[pl.ds(0, DP - 1)]
            pltpu.make_async_copy(others, others, raw_recv.at[stage]).wait()

        def unpack_raw(j, total):
            one = combine(recv_g[2 * j], recv_m[2 * j])[1].astype(BF16).astype(F32)
            two = combine(recv_g[2 * j + 1], recv_m[2 * j + 1])[1].astype(BF16).astype(F32)
            return unpack(one, two, j, 0, total)

        squared = lax.fori_loop(0, DP // 2, unpack_raw, jnp.zeros((8, 128), F32), unroll=4)
        for low, cols, new in grams(pl.ds(*GATHER[0])):
            acc[low, cols] = new

        for c in (*range(2, len(GATHER)), 1):
            landing = recvs[c - 1]
            arriving = landing.at[pl.ds(0, DP if c == 1 else DP - 1)]
            pltpu.make_async_copy(arriving, arriving, lead_recv.at[c - 1]).wait()

            def unpack_lead(j, total, landing=landing, start=GATHER[c][0]):
                return unpack(landing[2 * j].astype(F32), landing[2 * j + 1].astype(F32), j, start, total)

            squared = lax.fori_loop(0, DP // 2, unpack_lead, squared, unroll=4)
            for low, cols, new in grams(pl.ds(*GATHER[c])):
                acc[low, cols] += new

        norm = jnp.sqrt(jnp.sum(squared, axis=(0, 1), keepdims=True)) + epsilon
        inverse = 1.0 / norm

        def put(ref, n, value):
            value = value.astype(BF16)
            low, cols = lower(n)
            ref[low, cols] = value
            for m in range(n + 1, 3):
                ref[cols, pl.ds(256 * m, 256)] = value[256 * (m - n) : 256 * (m - n) + 256].T

        def product(left, right, n):
            low, cols = lower(n)
            return jnp.dot(left[low, :], right[:, cols], preferred_element_type=F32)

        def block(ref, n):
            return ref[lower(n)].astype(F32)

        for n in range(3):
            put(gram, n, acc[lower(n)] * inverse * inverse)
        for n in range(3):
            put(mix, n, cub_coef * block(gram, n) + quint_coef * product(gram, gram, n))
        for n in range(3):
            new = product(mix, gram, n)
            put(prod, n, new)
            acc[lower(n)] = lin_coef * lin_coef * block(gram, n) + 2.0 * lin_coef * new
        for n in range(3):
            put(gram, n, acc[lower(n)] + product(mix, prod, n))
        for n in range(3):
            put(mix2, n, cub_coef * block(gram, n) + quint_coef * product(gram, gram, n))
        for n in range(3):
            put(prod, n, lin_coef * (block(mix, n) + block(mix2, n)) + product(mix2, mix, n))

        scale = inverse * (0.2 * math.sqrt(max(FULL, WIDTH)))

        for c, (start, width) in enumerate(SPREAD):
            half = width // 2
            parts = []
            for columns in (pl.ds(start, half), pl.ds(start + half, half)):
                right = full[:, columns]
                new = jnp.dot(prod[...], right, preferred_element_type=F32)
                parts.append((new + lin_coef * lin_coef * right.astype(F32)) * scale)
            for d in range(DP):
                rows = slice(d * ROWS, (d + 1) * ROWS)
                outgoing[c][d] = jnp.concatenate([part[rows] for part in parts], axis=0).astype(BF16)

            if c != AROUND:
                returned[c][my_k] = outgoing[c][me]

            def send(i, carry, c=c):
                dest = lax.rem(me + i, DP)
                if c == AROUND:
                    landing, sem = bouncing.at[(my_t - 1) * SIDE + my_x], bounce_recv
                else:
                    landing, sem = returned[c].at[my_k], ret_recv.at[c]
                pltpu.make_async_remote_copy(
                    src_ref=outgoing[c].at[dest], dst_ref=landing, send_sem=ret_send.at[c], recv_sem=sem,
                    device_id=(shifted(z, my_t, lax.rem(dest, 2), 1) if c == AROUND else z, dest), device_id_type=MESH,
                ).start()
                return carry

            lax.fori_loop(0 if c == AROUND else 1, DP, send, 0, unroll=True)

    pltpu.make_async_copy(bouncing, bouncing, bounce_recv).wait()

    def bounce(i, carry):
        t = i // SIDE + 1
        pltpu.make_async_remote_copy(
            src_ref=bouncing.at[i], dst_ref=returned[AROUND].at[lax.rem(i, SIDE) * (SIDE - 1) + t - 1], send_sem=bounce_send,
            recv_sem=ret_recv.at[AROUND], device_id=(shifted(z, t, core, -1), me), device_id_type=MESH,
        ).start()
        return carry

    lax.fori_loop(0, MATS, bounce, 0)

    stores = []
    for c in sorted(range(len(SPREAD)), key=lambda c: c == AROUND):
        start, width = SPREAD[c]
        landing = returned[c]

        if c == AROUND:
            pltpu.make_async_copy(landing, landing, ret_recv.at[c]).wait()
        else:

            @pl.when(is_owner)
            def _():
                others = landing.at[pl.ds(0, MATS - 1)]
                pltpu.make_async_copy(others, others, ret_recv.at[c]).wait()

            @pl.when(jnp.logical_not(is_owner))
            def _():
                pltpu.make_async_copy(landing, landing, ret_recv.at[c]).wait()

        def unpack_result(k, carry, landing=landing, start=start, half=width // 2):
            piece = landing[k].astype(F32)
            up_v[k, :, pl.ds(start, half)] = piece[:ROWS].astype(BF16)
            up_v[k, :, pl.ds(start + half, half)] = piece[ROWS:].astype(BF16)
            return carry

        lax.fori_loop(0, MATS, unpack_result, 0, unroll=4)
        columns = pl.ds(start, width)
        stores.append(pltpu.make_async_copy(up_v.at[:, :, columns], up_hbm.at[:, :, columns], out_sem.at[1 + c]))
        stores[-1].start()

    for stage, part in ((0, part_a), (1, part_b)):
        others = part.at[pl.ds(0, SUM_PEERS - 1)]
        pltpu.make_async_copy(others, others, sum_send.at[stage]).wait()

    @pl.when(is_owner)
    def _():
        others = raw.at[pl.ds(0, 2 * (MATS - 1))]
        pltpu.make_async_copy(others, others, raw_send).wait()
        for c, buffer in enumerate(leads):
            sent = buffer.at[pl.ds(0, MATS if c == 0 else MATS - 1)]
            pltpu.make_async_copy(sent, sent, lead_send.at[c]).wait()
        for c, buffer in enumerate(outgoing):
            sent = buffer.at[pl.ds(0, DP if c == AROUND else DP - 1)]
            pltpu.make_async_copy(sent, sent, ret_send.at[c]).wait()

    @pl.when(jnp.logical_not(is_owner))
    def _():
        pltpu.make_async_copy(raw, raw, raw_send).wait()
        for c, buffer in enumerate(leads):
            pltpu.make_async_copy(buffer, buffer, lead_send.at[c]).wait()

    @pl.when(my_t == 0)
    def _():
        pltpu.make_async_copy(passing, passing, pass_send).wait()

    pltpu.make_async_copy(bouncing, bouncing, bounce_send).wait()
    store_nm.wait()
    for store in stores:
        store.wait()


def shards(grads, momentum):
    shape = grads.shape
    flat = (MATS, ROWS, WIDTH)
    out = jax.ShapeDtypeStruct(flat, BF16)
    square = (FULL, FULL)
    new_momentum, update = pl.pallas_call(
        kernel,
        out_shape=(out, out),
        in_specs=[pl.BlockSpec(memory_space=pl.ANY)] * 2,
        out_specs=(pl.BlockSpec(memory_space=pl.ANY),) * 2,
        scratch_shapes=[
            pltpu.VMEM(flat, BF16),
            pltpu.VMEM(flat, BF16),
            pltpu.VMEM(flat, BF16),
            pltpu.VMEM(flat, BF16),
            pieces(2 * MATS, NARROW),
            pieces(DP, NARROW),
            pieces(DP, NARROW),
            [pieces(MATS, width) for _, width in GATHER[1:]],
            [pieces(DP, width) for _, width in GATHER[1:]],
            pltpu.VMEM((FULL, WIDTH), BF16),
            pltpu.VMEM(square, F32),
            pltpu.VMEM(square, BF16),
            pltpu.VMEM(square, BF16),
            pltpu.VMEM(square, BF16),
            pltpu.VMEM(square, BF16),
            [pieces(DP, width) for _, width in SPREAD],
            [pieces(MATS, width) for _, width in SPREAD],
            pltpu.VMEM((SIDE - 1, CHIPS, PIECE, NARROW // 2), BF16),
            pieces(MATS, NARROW),
            pltpu.VMEM((SUM_PEERS, 8, 128), F32),
            pltpu.VMEM((SUM_PEERS, 8, 128), F32),
            pltpu.SemaphoreType.DMA((4,)),
            pltpu.SemaphoreType.DMA,
            pltpu.SemaphoreType.DMA((1 + len(SPREAD),)),
            pltpu.SemaphoreType.DMA((2,)),
            pltpu.SemaphoreType.DMA((2,)),
            pltpu.SemaphoreType.DMA,
            pltpu.SemaphoreType.DMA((2,)),
            pltpu.SemaphoreType.DMA((len(GATHER) - 1,)),
            pltpu.SemaphoreType.DMA((len(GATHER) - 1,)),
            pltpu.SemaphoreType.DMA((len(SPREAD),)),
            pltpu.SemaphoreType.DMA((len(SPREAD),)),
            pltpu.SemaphoreType.DMA,
            pltpu.SemaphoreType.DMA((SIDE - 1,)),
            pltpu.SemaphoreType.DMA,
            pltpu.SemaphoreType.DMA,
        ],
        compiler_params=pltpu.CompilerParams(
            collective_id=0, has_side_effects=True, vmem_limit_bytes=51 * 1024 * 1024 + 256 * 1024
        ),
        name="muon_step",
    )(grads.reshape(flat), momentum.reshape(flat))
    return new_momentum.reshape(shape), update.reshape(shape)


def solution(mesh):
    placed = (P("expert", None, "dp", None), P("expert", None, "dp", None))
    return jax.shard_map(
        shards,
        mesh=mesh,
        in_specs=placed,
        out_specs=(P("expert", None, "dp", None), P("expert", None, "dp", None)),
        check_vma=False,
    )
```

```python
import functools
import math

import jax
import jax.numpy as jnp
from jax import lax
from jax.experimental import pallas as pl
from jax.experimental.pallas import tpu as pltpu
from jax.sharding import PartitionSpec as P

lin_coef = 3.4445
cub_coef = -4.775
quint_coef = 2.0315
epsilon = 1e-07
momentum_rate = 0.95

MESH = pl.DeviceIdType.MESH
F32 = jnp.float32
BF16 = jnp.bfloat16

SIDE = 4
CHIPS = SIDE * SIDE
PLANES = 8
DP = 2 * CHIPS
MATS = 12
ROWS = 24
WIDTH = 2048
FULL = ROWS * DP
COLS = 512
NARROW = 256
PIECE = 2 * ROWS
SUM_PEERS = 16
GATHER = ((0, NARROW), (NARROW, NARROW), (512, COLS), (1024, COLS), (1536, COLS))
SPREAD = ((0, NARROW), (NARROW, NARROW), (512, COLS), (1024, COLS), (1536, COLS))
AROUND = 1


def hops(step, size):
    return min(step, size - step)


FAR_A = sorted(
    ((dz, other) for dz in range(PLANES) for other in range(2) if dz or other), key=lambda p: -hops(p[0], PLANES)
)
FAR_B = sorted(
    ((dy, dx) for dy in range(SIDE) for dx in range(SIDE) if dy or dx),
    key=lambda p: -hops(p[0], SIDE) - hops(p[1], SIDE),
)


def owner_of(k, z):
    x = k // (SIDE - 1)
    y = lax.rem(x + z + 1 + lax.rem(k, SIDE - 1), SIDE)
    return (y * SIDE + x) * 2


def shifted(z, t, core, sign):
    step = jnp.where(t == 1, 1, jnp.where(t == 2, 2 - 4 * core, -1))
    return lax.rem(z + PLANES + sign * step, PLANES)


def stack_halves(wide):
    half = wide.shape[1] // 2
    return jnp.concatenate([wide[:, :half], wide[:, half:]], axis=0)


def pieces(count, columns):
    return pltpu.VMEM((count, PIECE, columns // 2), BF16)


def kernel(
    g_hbm, m_hbm, nm_hbm, up_hbm,
    g_v, m_v, nm_v, up_v, raw, recv_g, recv_m, leads, recvs, full, acc, gram, mix, prod, mix2, outgoing, returned, passing, bouncing, part_a, part_b,
    g_sem, m_sem, out_sem, sum_send, sum_recv, raw_send, raw_recv, lead_send, lead_recv, ret_send, ret_recv, pass_send, pass_recv, bounce_send, bounce_recv,
):
    z = lax.axis_index("expert")
    me = lax.axis_index("dp")
    chip = me // 2
    core = lax.rem(me, 2)
    my_y = chip // SIDE
    my_x = lax.rem(chip, SIDE)
    my_t = lax.rem(my_y - my_x - z + 3 * SIDE, SIDE)
    is_owner = jnp.logical_and(core == 0, my_t != 0)
    my_k = my_x * (SIDE - 1) + my_t - 1

    line = z * 2 + core

    def peer_a(i):
        dz, other = FAR_A[i - 1]
        return (lax.rem(z + dz, PLANES), chip * 2 + (1 - core if other else core))

    def peer_b(i):
        dy, dx = FAR_B[i - 1]
        return (z, (lax.rem(my_y + dy, SIDE) * SIDE + lax.rem(my_x + dx, SIDE)) * 2 + core)

    for k in range(4):
        part = pl.ds(3 * k, 3)
        pltpu.make_async_copy(g_hbm.at[part], g_v.at[part], g_sem.at[k]).start()
    load_m = pltpu.make_async_copy(m_hbm, m_v, m_sem)

    barrier = pltpu.get_barrier_semaphore()
    for i in range(1, SUM_PEERS):
        pl.semaphore_signal(barrier, inc=1, device_id=peer_a(i), device_id_type=MESH)
        pl.semaphore_signal(barrier, inc=1, device_id=peer_b(i), device_id_type=MESH)

    @pl.when(is_owner)
    def _():
        for i in range(1, CHIPS):
            other = (z, lax.rem(chip + i, CHIPS) * 2 + 1)
            pl.semaphore_signal(barrier, inc=1, device_id=other, device_id_type=MESH)

    total = jnp.zeros((8, 128), F32)
    for k in range(4):
        part = pl.ds(3 * k, 3)
        pltpu.make_async_copy(g_hbm.at[part], g_v.at[part], g_sem.at[k]).wait()

        def squares(i, carry):
            wide = g_v[i // 4, :, pl.ds(pl.multiple_of(lax.rem(i, 4) * COLS, COLS), COLS)].astype(F32)
            wide = wide * wide
            wide = wide[0:8] + wide[8:16] + wide[16:24]
            wide = wide[:, 0:256] + wide[:, 256:512]
            return carry + (wide[:, 0:128] + wide[:, 128:256])

        if k == 3:
            load_m.start()
        total = lax.fori_loop(12 * k, 12 * k + 12, squares, total, unroll=4)

    others_owning = jnp.where(my_t != 0, MATS - 1, MATS)
    pl.semaphore_wait(barrier, 2 * (SUM_PEERS - 1) + jnp.where(core == 1, others_owning, 0))

    def send_sum(total, part, slot, peer, stage):
        part[slot] = total
        for i in range(1, SUM_PEERS):
            pltpu.make_async_remote_copy(
                src_ref=part.at[slot], dst_ref=part.at[slot], send_sem=sum_send.at[stage], recv_sem=sum_recv.at[stage],
                device_id=peer(i), device_id_type=MESH,
            ).start()

    def take_sum(part, stage):
        others = part.at[pl.ds(0, SUM_PEERS - 1)]
        pltpu.make_async_copy(others, others, sum_recv.at[stage]).wait()
        return jnp.sum(part[...], axis=0)

    def push(piece, buffer, slot, landing, k, send_sem, recv_sem):
        dest = owner_of(k, z)
        buffer[slot] = piece

        @pl.when(dest == me)
        def _():
            landing[me] = piece

        @pl.when(dest != me)
        def _():
            pltpu.make_async_remote_copy(
                src_ref=buffer.at[slot], dst_ref=landing.at[me], send_sem=send_sem, recv_sem=recv_sem,
                device_id=(z, dest), device_id_type=MESH,
            ).start()

    send_sum(total, part_a, line, peer_a, 0)
    load_m.wait()

    def send_raw(i, carry):
        k = lax.rem(i + me, MATS)
        push(stack_halves(g_v[k, :, :NARROW].astype(F32)).astype(BF16), raw, k, recv_g, k, raw_send, raw_recv.at[0])
        push(stack_halves(m_v[k, :, :NARROW].astype(F32)).astype(BF16), raw, MATS + k, recv_m, k, raw_send, raw_recv.at[1])
        return carry

    lax.fori_loop(0, MATS, send_raw, 0)
    total = take_sum(part_a, 0)
    send_sum(total, part_b, chip, peer_b, 1)
    total = take_sum(part_b, 1)
    count = MATS * PLANES * FULL * WIDTH
    mean = jnp.sum(total, axis=(0, 1), keepdims=True) / count
    clip = 1.0 / jnp.maximum(jnp.sqrt(mean), 1.0)

    def combine(g, m):
        scaled = clip * g.astype(F32)
        moment = momentum_rate * m.astype(F32) + scaled
        return moment, scaled + momentum_rate * moment

    def send_around(i, carry):
        k = lax.rem(i + me, MATS)
        t = lax.rem(k, SIDE - 1) + 1
        columns = pl.ds(*GATHER[1])
        leads[0][k] = stack_halves(combine(g_v[k, :, columns], m_v[k, :, columns])[1]).astype(BF16)
        pltpu.make_async_remote_copy(
            src_ref=leads[0].at[k], dst_ref=passing.at[t - 1, chip], send_sem=lead_send.at[0],
            recv_sem=pass_recv.at[t - 1], device_id=(shifted(z, t, core, 1), owner_of(k, z) + core), device_id_type=MESH,
        ).start()
        return carry

    for c in range(2, len(GATHER)):
        columns = pl.ds(*GATHER[c])

        def send_lead(i, carry, columns=columns, c=c):
            if c == 2:
                send_around(i, carry)
            k = lax.rem(i + me, MATS)
            piece = stack_halves(combine(g_v[k, :, columns], m_v[k, :, columns])[1]).astype(BF16)
            push(piece, leads[c - 1], k, recvs[c - 1], k, lead_send.at[c - 1], lead_recv.at[c - 1])
            return carry

        lax.fori_loop(0, MATS, send_lead, 0, unroll=2)

    @pl.when(my_t == 0)
    def _():
        for t in (2, 1, 3):
            every = passing.at[t - 1]
            pltpu.make_async_copy(every, every, pass_recv.at[t - 1]).wait()

            def hand_on(i, carry, t=t):
                source = lax.rem(i + chip, CHIPS)
                pltpu.make_async_remote_copy(
                    src_ref=passing.at[t - 1, source], dst_ref=recvs[0].at[source * 2 + core], send_sem=pass_send,
                    recv_sem=lead_recv.at[0], device_id=(shifted(z, t, core, -1), chip * 2), device_id_type=MESH,
                ).start()
                return carry

            lax.fori_loop(0, CHIPS, hand_on, 0)

    def momentum_step(i, carry):
        k = i // 4
        columns = pl.ds(pl.multiple_of(lax.rem(i, 4) * COLS, COLS), COLS)
        nm_v[k, :, columns] = combine(g_v[k, :, columns], m_v[k, :, columns])[0].astype(BF16)
        return carry

    lax.fori_loop(0, 4 * MATS, momentum_step, 0, unroll=4)
    store_nm = pltpu.make_async_copy(nm_v, nm_hbm, out_sem.at[0])
    store_nm.start()

    @pl.when(is_owner)
    def _():
        def unpack(one, two, j, start, total):
            half = one.shape[1]
            rows = pl.ds(pl.multiple_of(j * PIECE, PIECE), PIECE)
            full[rows, pl.ds(start, half)] = jnp.concatenate([one[:ROWS], two[:ROWS]], axis=0).astype(BF16)
            full[rows, pl.ds(start + half, half)] = jnp.concatenate([one[ROWS:], two[ROWS:]], axis=0).astype(BF16)
            both = one * one + two * two
            if half == 256:
                both = both[:, :128] + both[:, 128:]
            return total + (both[0:8] + both[8:16] + both[16:24] + both[24:32] + both[32:40] + both[40:48])

        def lower(n):
            return pl.ds(256 * n, FULL - 256 * n), pl.ds(256 * n, 256)

        def grams(columns):
            for n in range(3):
                low, cols = lower(n)
                new = lax.dot_general(
                    full[low, columns], full[cols, columns], (((1,), (1,)), ((), ())), preferred_element_type=F32
                )
                yield low, cols, new

        for stage, landing in ((0, recv_g), (1, recv_m)):
            others = landing.at[pl.ds(0, DP - 1)]
            pltpu.make_async_copy(others, others, raw_recv.at[stage]).wait()

        def unpack_raw(j, total):
            one = combine(recv_g[2 * j], recv_m[2 * j])[1].astype(BF16).astype(F32)
            two = combine(recv_g[2 * j + 1], recv_m[2 * j + 1])[1].astype(BF16).astype(F32)
            return unpack(one, two, j, 0, total)

        squared = lax.fori_loop(0, DP // 2, unpack_raw, jnp.zeros((8, 128), F32), unroll=4)
        for low, cols, new in grams(pl.ds(*GATHER[0])):
            acc[low, cols] = new

        for c in (*range(2, len(GATHER)), 1):
            landing = recvs[c - 1]
            arriving = landing.at[pl.ds(0, DP if c == 1 else DP - 1)]
            pltpu.make_async_copy(arriving, arriving, lead_recv.at[c - 1]).wait()

            def unpack_lead(j, total, landing=landing, start=GATHER[c][0]):
                return unpack(landing[2 * j].astype(F32), landing[2 * j + 1].astype(F32), j, start, total)

            squared = lax.fori_loop(0, DP // 2, unpack_lead, squared, unroll=4)
            for low, cols, new in grams(pl.ds(*GATHER[c])):
                acc[low, cols] += new

        norm = jnp.sqrt(jnp.sum(squared, axis=(0, 1), keepdims=True)) + epsilon
        inverse = 1.0 / norm

        def put(ref, n, value):
            value = value.astype(BF16)
            low, cols = lower(n)
            ref[low, cols] = value
            for m in range(n + 1, 3):
                ref[cols, pl.ds(256 * m, 256)] = value[256 * (m - n) : 256 * (m - n) + 256].T

        def product(left, right, n):
            low, cols = lower(n)
            return jnp.dot(left[low, :], right[:, cols], preferred_element_type=F32)

        def block(ref, n):
            return ref[lower(n)].astype(F32)

        for n in range(3):
            put(gram, n, acc[lower(n)] * inverse * inverse)
        for n in range(3):
            put(mix, n, cub_coef * block(gram, n) + quint_coef * product(gram, gram, n))
        for n in range(3):
            new = product(mix, gram, n)
            put(prod, n, new)
            acc[lower(n)] = lin_coef * lin_coef * block(gram, n) + 2.0 * lin_coef * new
        for n in range(3):
            put(gram, n, acc[lower(n)] + product(mix, prod, n))
        for n in range(3):
            put(mix2, n, cub_coef * block(gram, n) + quint_coef * product(gram, gram, n))
        for n in range(3):
            put(prod, n, lin_coef * (block(mix, n) + block(mix2, n)) + product(mix2, mix, n))

        scale = inverse * (0.2 * math.sqrt(max(FULL, WIDTH)))

        for c, (start, width) in enumerate(SPREAD):
            half = width // 2
            parts = []
            for first in range(start, start + width, 256):
                right = full[:, pl.ds(first, 256)]
                new = jnp.dot(prod[...], right, preferred_element_type=F32)
                new = (new + lin_coef * lin_coef * right.astype(F32)) * scale
                parts.extend((new[:, :half], new[:, half:]) if half < 256 else (new,))
            for d in range(DP):
                rows = slice(d * ROWS, (d + 1) * ROWS)
                outgoing[c][d] = jnp.concatenate([part[rows] for part in parts], axis=0).astype(BF16)

            if c != AROUND:
                returned[c][my_k] = outgoing[c][me]

            def send(i, carry, c=c):
                dest = lax.rem(me + i, DP)
                if c == AROUND:
                    landing, sem = bouncing.at[(my_t - 1) * SIDE + my_x], bounce_recv
                else:
                    landing, sem = returned[c].at[my_k], ret_recv.at[c]
                pltpu.make_async_remote_copy(
                    src_ref=outgoing[c].at[dest], dst_ref=landing, send_sem=ret_send.at[c], recv_sem=sem,
                    device_id=(shifted(z, my_t, lax.rem(dest, 2), 1) if c == AROUND else z, dest), device_id_type=MESH,
                ).start()
                return carry

            lax.fori_loop(0 if c == AROUND else 1, DP, send, 0, unroll=True)

    pltpu.make_async_copy(bouncing, bouncing, bounce_recv).wait()

    def bounce(i, carry):
        t = i // SIDE + 1
        pltpu.make_async_remote_copy(
            src_ref=bouncing.at[i], dst_ref=returned[AROUND].at[lax.rem(i, SIDE) * (SIDE - 1) + t - 1], send_sem=bounce_send,
            recv_sem=ret_recv.at[AROUND], device_id=(shifted(z, t, core, -1), me), device_id_type=MESH,
        ).start()
        return carry

    lax.fori_loop(0, MATS, bounce, 0)

    stores = []
    for c in sorted(range(len(SPREAD)), key=lambda c: c == AROUND):
        start, width = SPREAD[c]
        landing = returned[c]

        if c == AROUND:
            pltpu.make_async_copy(landing, landing, ret_recv.at[c]).wait()
        else:

            @pl.when(is_owner)
            def _():
                others = landing.at[pl.ds(0, MATS - 1)]
                pltpu.make_async_copy(others, others, ret_recv.at[c]).wait()

            @pl.when(jnp.logical_not(is_owner))
            def _():
                pltpu.make_async_copy(landing, landing, ret_recv.at[c]).wait()

        def unpack_result(k, carry, landing=landing, start=start, half=width // 2):
            piece = landing[k].astype(F32)
            up_v[k, :, pl.ds(start, half)] = piece[:ROWS].astype(BF16)
            up_v[k, :, pl.ds(start + half, half)] = piece[ROWS:].astype(BF16)
            return carry

        lax.fori_loop(0, MATS, unpack_result, 0, unroll=4)
        columns = pl.ds(start, width)
        stores.append(pltpu.make_async_copy(up_v.at[:, :, columns], up_hbm.at[:, :, columns], out_sem.at[1 + c]))
        stores[-1].start()

    for stage, part in ((0, part_a), (1, part_b)):
        others = part.at[pl.ds(0, SUM_PEERS - 1)]
        pltpu.make_async_copy(others, others, sum_send.at[stage]).wait()

    @pl.when(is_owner)
    def _():
        others = raw.at[pl.ds(0, 2 * (MATS - 1))]
        pltpu.make_async_copy(others, others, raw_send).wait()
        for c, buffer in enumerate(leads):
            sent = buffer.at[pl.ds(0, MATS if c == 0 else MATS - 1)]
            pltpu.make_async_copy(sent, sent, lead_send.at[c]).wait()
        for c, buffer in enumerate(outgoing):
            sent = buffer.at[pl.ds(0, DP if c == AROUND else DP - 1)]
            pltpu.make_async_copy(sent, sent, ret_send.at[c]).wait()

    @pl.when(jnp.logical_not(is_owner))
    def _():
        pltpu.make_async_copy(raw, raw, raw_send).wait()
        for c, buffer in enumerate(leads):
            pltpu.make_async_copy(buffer, buffer, lead_send.at[c]).wait()

    @pl.when(my_t == 0)
    def _():
        pltpu.make_async_copy(passing, passing, pass_send).wait()

    pltpu.make_async_copy(bouncing, bouncing, bounce_send).wait()
    store_nm.wait()
    for store in stores:
        store.wait()


def shards(grads, momentum):
    shape = grads.shape
    flat = (MATS, ROWS, WIDTH)
    out = jax.ShapeDtypeStruct(flat, BF16)
    square = (FULL, FULL)
    new_momentum, update = pl.pallas_call(
        kernel,
        out_shape=(out, out),
        in_specs=[pl.BlockSpec(memory_space=pl.ANY)] * 2,
        out_specs=(pl.BlockSpec(memory_space=pl.ANY),) * 2,
        scratch_shapes=[
            pltpu.VMEM(flat, BF16),
            pltpu.VMEM(flat, BF16),
            pltpu.VMEM(flat, BF16),
            pltpu.VMEM(flat, BF16),
            pieces(2 * MATS, NARROW),
            pieces(DP, NARROW),
            pieces(DP, NARROW),
            [pieces(MATS, width) for _, width in GATHER[1:]],
            [pieces(DP, width) for _, width in GATHER[1:]],
            pltpu.VMEM((FULL, WIDTH), BF16),
            pltpu.VMEM(square, F32),
            pltpu.VMEM(square, BF16),
            pltpu.VMEM(square, BF16),
            pltpu.VMEM(square, BF16),
            pltpu.VMEM(square, BF16),
            [pieces(DP, width) for _, width in SPREAD],
            [pieces(MATS, width) for _, width in SPREAD],
            pltpu.VMEM((SIDE - 1, CHIPS, PIECE, NARROW // 2), BF16),
            pieces(MATS, NARROW),
            pltpu.VMEM((SUM_PEERS, 8, 128), F32),
            pltpu.VMEM((SUM_PEERS, 8, 128), F32),
            pltpu.SemaphoreType.DMA((4,)),
            pltpu.SemaphoreType.DMA,
            pltpu.SemaphoreType.DMA((1 + len(SPREAD),)),
            pltpu.SemaphoreType.DMA((2,)),
            pltpu.SemaphoreType.DMA((2,)),
            pltpu.SemaphoreType.DMA,
            pltpu.SemaphoreType.DMA((2,)),
            pltpu.SemaphoreType.DMA((len(GATHER) - 1,)),
            pltpu.SemaphoreType.DMA((len(GATHER) - 1,)),
            pltpu.SemaphoreType.DMA((len(SPREAD),)),
            pltpu.SemaphoreType.DMA((len(SPREAD),)),
            pltpu.SemaphoreType.DMA,
            pltpu.SemaphoreType.DMA((SIDE - 1,)),
            pltpu.SemaphoreType.DMA,
            pltpu.SemaphoreType.DMA,
        ],
        compiler_params=pltpu.CompilerParams(
            collective_id=0, has_side_effects=True, vmem_limit_bytes=51 * 1024 * 1024 + 256 * 1024
        ),
        name="muon_step",
    )(grads.reshape(flat), momentum.reshape(flat))
    return new_momentum.reshape(shape), update.reshape(shape)


def solution(mesh):
    placed = (P("expert", None, "dp", None), P("expert", None, "dp", None))
    return jax.shard_map(
        shards,
        mesh=mesh,
        in_specs=placed,
        out_specs=(P("expert", None, "dp", None), P("expert", None, "dp", None)),
        check_vma=False,
    )
```
